256 devices in a mesh: ppl: 8 (over y_hi, x), snp: 32 (over y_lo, z, core).
Axes of the slice: x: 4, y: 4 (y_hi: 2, y_lo: 2; y = y_hi * 2 + y_lo), z: 8, core: 2. Of those that a mesh axis runs over, the one named last changes fastest.
Arguments:
- genotypes: bfloat16 [30720, 32768], P('ppl', 'snp'), may hold values from -0.03125 to 0.03125
- residual: float32 [64, 30720], P(None, 'ppl'), may hold values from -130 to 130
- effects: float32 [64, 32768], P(None, 'snp'), may hold values from -3 to 3
- assignments: int32 [32768], P('snp'), may hold values from 0 to 3
- ld_blocks: float32 [256, 128, 128], P('snp'), may hold values from -0.15 to 1.6, as said below
- ld_inverses: float32 [256, 128, 128], P('snp'), may hold values from -0.15 to 1.6, as said below
- ld_factors: float32 [256, 128, 128], P('snp'), may hold values from -0.15 to 1.2
- normals: float32 [2, 64, 32768], P(None, None, 'snp'), may hold values from -6 to 6
Outputs:
- effects_out: float32 [64, 32768], P(None, 'snp')
- residual_out: float32 [64, 30720], P(None, 'ppl')
The draws below stay inside these ranges and needn't reach their ends.
Inputs may be any that keep to these rules, and one draw needn't show every extreme that they name: `ld_blocks`: symmetric. `ld_inverses`: symmetric.
All inputs are finite; a program needn't handle non-finite values.
Results may differ from the reference program's by a relative error of at most 0.0003.
Values sent between devices are 32-bit elements; how exact they have to be, the bound alone decides.
A program may use at most 128 MiB of HBM per device.

```python
import math
import jax
import jax.numpy as jnp
from jax import lax

TRAITS = 64
BLOCK = 128
BLOCKS_DEV = 8
SWEEPS = 2
SNP_DEV = 1024
GROUPS = 32
SNPS = 32768
BLOCKS = 256
PEOPLE = 30720


def symmetric_blocks(key, diag_low, diag_high, off_size):
    key_diag, key_off = jax.random.split(key)
    diagonal = jax.random.uniform(key_diag, (BLOCKS, BLOCK), jnp.float32, diag_low, diag_high)
    raw = jax.random.uniform(key_off, (BLOCKS, BLOCK, BLOCK), jnp.float32, -off_size, off_size)
    mirrored = 0.5 * (raw + jnp.swapaxes(raw, 1, 2))
    identity = jnp.eye(BLOCK, dtype=jnp.float32)
    return mirrored * (1.0 - identity)[None] + identity[None] * diagonal[:, :, None]


def lower_blocks(key, diag_low, diag_high, off_size):
    key_diag, key_off = jax.random.split(key)
    diagonal = jax.random.uniform(key_diag, (BLOCKS, BLOCK), jnp.float32, diag_low, diag_high)
    raw = jax.random.uniform(key_off, (BLOCKS, BLOCK, BLOCK), jnp.float32, -off_size, off_size)
    below = jnp.tril(jnp.ones((BLOCK, BLOCK), jnp.float32), -1)
    identity = jnp.eye(BLOCK, dtype=jnp.float32)
    return raw * below[None] + identity[None] * diagonal[:, :, None]


def draw_ld_blocks(key, part):
    key = jax.random.fold_in(key, 5)
    return symmetric_blocks(key, 0.6, 1.4, 0.1)


def draw_ld_inverses(key, part):
    key = jax.random.fold_in(key, 7)
    return symmetric_blocks(key, 0.45, 0.95, 0.1)


def draw_ld_factors(key, part):
    key = jax.random.fold_in(key, 13)
    return lower_blocks(key, 0.5, 1.0, 0.1)


def draw_residual(key, part):
    key = jax.random.fold_in(key, 11)
    key_rows, key_cols, key_base = jax.random.split(key, 3)
    place = jnp.arange(PEOPLE, dtype=jnp.float32) / max(PEOPLE - 1, 1)
    row_scale = jnp.exp(jax.random.uniform(key_rows, (PEOPLE,), jnp.float32, 0.0, 0.5 * math.log(10.0)))
    col_scale = jnp.exp(jax.random.uniform(key_cols, (TRAITS,), jnp.float32, math.log(0.5), math.log(1.6)))
    base = jnp.clip(jax.random.normal(key_base, (TRAITS, PEOPLE), jnp.float32), -6.0, 6.0)
    ramp = jnp.exp(place * 0.5 * math.log(3.0))
    return col_scale[:, None] * (ramp * row_scale)[None, :] * base


def with_ends(values, stream_key, smallest, high):
    spot = [jax.random.randint(jax.random.fold_in(stream_key, axis), (), 0, length) for axis, length in enumerate(values.shape)]
    widest = values.shape.index(max(values.shape))
    beside = spot[:widest] + [(spot[widest] + 1) % values.shape[widest]] + spot[widest + 1:]
    return values.at[tuple(spot)].set(smallest).at[tuple(beside)].set(high)


def shard_levels(stream_key, extent, cuts, smallest, top_value):
    def one(dim, shards_of):
        steps = jax.random.uniform(jax.random.fold_in(jax.random.fold_in(stream_key, 6), dim), (shards_of,), jnp.float32, smallest / len(cuts), top_value / len(cuts))
        return jnp.repeat(jnp.exp(steps), extent[dim] // shards_of).reshape((-1,) + (1,) * (len(extent) - dim - 1))

    level = one(*cuts[0])
    for cut in cuts[1:]:
        level = level * one(*cut)
    return level


def gaussian(rng, extent, scale, bound, pieces=(), held_as=jnp.bfloat16):
    drawn = jax.random.normal(rng, extent, jnp.float32) * scale
    if len(pieces) > 0:
        drawn = shard_levels(rng, extent, pieces, -0.22, 0.18) * drawn
    return jnp.clip(drawn, min=-bound, max=bound).astype(held_as)


def setup_inputs(seed: int = 0) -> dict:
    seeds = jax.random.split(jax.random.key(seed), 9)
    return {
        "genotypes": gaussian(seeds[0], (PEOPLE, SNPS), PEOPLE ** -0.5, 0.03125, ((0, 8), (1, 32))),
        "residual": draw_residual(jax.random.fold_in(seeds[8], 71), 0),
        "effects": gaussian(seeds[2], (TRAITS, SNPS), 0.5, 3.0, ((1, 32),), jnp.float32),
        "assignments": with_ends(jax.random.randint(seeds[3], (SNPS,), 0, 4), jax.random.fold_in(seeds[3], 1), 0, 3).astype(jnp.int32),
        "ld_blocks": draw_ld_blocks(jax.random.fold_in(seeds[8], 71), 0),
        "ld_inverses": draw_ld_inverses(jax.random.fold_in(seeds[8], 71), 0),
        "ld_factors": draw_ld_factors(jax.random.fold_in(seeds[8], 71), 0),
        "normals": gaussian(seeds[7], (SWEEPS, TRAITS, SNPS), 1.0, 6.0, ((2, 32),), jnp.float32),
    }


SHRINK_FACTORS = (0.0, 0.3, 0.6, 1.0)
HIGH = lax.Precision.HIGHEST

def shrinkage(assignments):
    result = jnp.zeros(assignments.shape, jnp.float32)
    for component, factor in enumerate(SHRINK_FACTORS):
        result = result + jnp.where(assignments == component, jnp.float32(factor), jnp.float32(0.0))
    return result

def reference(genotypes, residual, effects, assignments, ld_blocks, ld_inverses, ld_factors, normals):
    shrink = shrinkage(assignments)
    for sweep in range(SWEEPS):
        spread = jnp.sqrt(lax.optimization_barrier(jnp.sum(residual * residual, axis=1)) / PEOPLE)
        draws = normals[sweep]
        current = residual
        betas = effects

        def one_group(total, group):
            delta = jnp.zeros((TRAITS, PEOPLE), jnp.float32)
            updated = []
            for block in range(BLOCKS_DEV):
                start = (group * SNP_DEV + block * BLOCK).astype(jnp.int32)
                index = (group * BLOCKS_DEV + block).astype(jnp.int32)
                columns = lax.dynamic_slice_in_dim(genotypes, start, BLOCK, 1).astype(jnp.float32)
                before = lax.dynamic_slice_in_dim(betas, start, BLOCK, 1)
                noise = lax.dynamic_slice_in_dim(draws, start, BLOCK, 1)
                factor = lax.dynamic_slice_in_dim(shrink, start, BLOCK, 0)
                ld_matrix = lax.dynamic_index_in_dim(ld_blocks, index, 0, keepdims=False)
                ld_inverse = lax.dynamic_index_in_dim(ld_inverses, index, 0, keepdims=False)
                ld_factor = lax.dynamic_index_in_dim(ld_factors, index, 0, keepdims=False)
                rhs = jnp.einsum('kp,pb->kb', current - delta, columns, precision=HIGH)
                rhs = rhs + jnp.einsum('kc,bc->kb', before, ld_matrix, precision=HIGH)
                mean = jnp.einsum('kc,bc->kb', rhs, ld_inverse, precision=HIGH)
                jitter = jnp.einsum('kc,bc->kb', noise, ld_factor, precision=HIGH)
                after = factor[None, :] * (mean + spread[:, None] * jitter)
                delta = delta + jnp.einsum('kb,pb->kp', after - before, columns, precision=HIGH)
                updated.append(after)
            return (total + delta, jnp.concatenate(updated, axis=1))
        total, group_effects = lax.scan(one_group, jnp.zeros((TRAITS, PEOPLE), jnp.float32), jnp.arange(GROUPS, dtype=jnp.int32))
        effects = jnp.transpose(group_effects, (1, 0, 2)).reshape(TRAITS, SNPS)
        residual = residual - total
    return (effects, residual)
```

```python
import functools

import jax
import jax.numpy as jnp
from jax import lax
from jax.experimental import pallas as pl
from jax.experimental.pallas import tpu as pltpu
from jax.sharding import PartitionSpec as P

F32 = jnp.float32
BF16 = jnp.bfloat16
MESH = pl.DeviceIdType.MESH
HIGHEST = lax.Precision.HIGHEST
FACTORS = (0.0, 0.3, 0.6, 1.0)
TRAITS, ROWS, SNPS, BLOCK, NB = 64, 3840, 1024, 128, 8
TILES = 32
PAIRS = (
    [(p, q) for q in range(1, 4) for p in range(q)],
    [(p, q) for q in range(5, 8) for p in range(4, q)],
    [(p, q) for q in range(4, 8) for p in range(4)],
)


def ds(start, size):
    return pl.ds(pl.multiple_of(start, size), size)


def dot(a, b):
    return jnp.dot(a, b, preferred_element_type=F32)


def dot_nt(a, b, precision=None):
    return lax.dot_general(a, b, (((1,), (1,)), ((), ())), precision=precision, preferred_element_type=F32)


def dot_tn(a, b):
    return lax.dot_general(a, b, (((0,), (0,)), ((), ())), preferred_element_type=F32)


def split(x):
    high = x.astype(BF16)
    return high, (x - high.astype(F32)).astype(BF16)


def stacked(x):
    return jnp.concatenate(split(x), axis=0)


def dot3(a, b_high, b_low):
    n = a.shape[0]
    high, low = split(a)
    both = dot(jnp.concatenate([high, low], axis=0), b_high)
    return both[:n] + both[n:] + dot(high, b_low)


def kernel(
    people,
    x_hbm, r_hbm, e_hbm, a_ref, ld_hbm, inv_hbm, fac_hbm, n_hbm,
    e_out, r_out,
    xv, rv, ev, ldv, invv, facv, nv,
    rl, acc, rxs0, rxs1, rxs2, rxr0, rxr1, rxr2, rxl,
    gram_a, gram_b, gram_c, gr_a, gr_b, gr_c, ms_a, ms_b, ms_c, mr_a, mr_b, mr_c, gch, gcl, mh, ml, wh, wl, jit, lin,
    mine, everyone, chl, d, cr, yr, zr, rn,
    send_sem, recv_sem, local_sem,
):
    me = lax.axis_index("ppl")
    snp = lax.axis_index("snp")
    yh, xx = me // 4, lax.rem(me, 4)
    yl, zz, cc = snp // 16, lax.rem(snp // 2, 8), lax.rem(snp, 2)

    def on_ppl(j):
        return {"ppl": lax.rem(yh + j // 4, 2) * 4 + lax.rem(xx + j % 4, 4), "snp": snp}

    def on_z(j):
        return {"ppl": me, "snp": yl * 16 + lax.rem(zz + j, 8) * 2 + cc}

    on_y = {"ppl": me, "snp": (1 - yl) * 16 + zz * 2 + cc}
    on_core = {"ppl": me, "snp": yl * 16 + zz * 2 + 1 - cc}

    sends = []
    count = [0]

    def slots(n):
        first = count[0]
        count[0] += n
        return first

    def copy(src, dst, slot, device):
        return pltpu.make_async_remote_copy(
            src_ref=src, dst_ref=dst, send_sem=send_sem.at[slot], recv_sem=recv_sem.at[slot],
            device_id=device, device_id_type=MESH,
        )

    def start(src, dst, slot, device):
        c = copy(src, dst, slot, device)
        c.start()
        sends.append(c)
        return c

    def ppl_scatter(src_of, dst):
        base = slots(7)
        return [start(src_of(on_ppl(j)["ppl"]), dst.at[j - 1], base + j - 1, on_ppl(j)) for j in range(1, 8)]

    def ppl_gather(src, dst):
        base = slots(7)
        return [start(src, dst, base + j - 1, on_ppl(j)) for j in range(1, 8)]

    def arrived(copies):
        for c in copies:
            c.wait_recv()

    def load(i, src, dst):
        c = pltpu.make_async_copy(src, dst, local_sem.at[i])
        c.start()
        return c

    load_r = load(0, r_hbm, rv.at[:, 0:ROWS])
    load_x = []
    for g in range(4):
        top = min(1024 * g + 1024, ROWS)
        part = pl.ds(1024 * g, top - 1024 * g)
        load_x.append(load(1 + g, x_hbm.at[part, :], xv.at[part, :]))
    load_small = [
        load(5, inv_hbm, invv), load(6, fac_hbm, facv), load(7, n_hbm.at[:, ds(8 * me, 8), :], nv),
        load(8, ld_hbm, ldv), load(9, e_hbm, ev),
    ]
    xv[ROWS:4096, :] = jnp.zeros((4096 - ROWS, SNPS), BF16)
    rv[:, ROWS:4096] = jnp.zeros((TRAITS, 4096 - ROWS), F32)

    barrier = pltpu.get_barrier_semaphore()
    partners = [on_ppl(j) for j in range(1, 8)] + [on_z(j) for j in range(1, 8)] + [on_y, on_core]
    for device in partners:
        pl.semaphore_signal(barrier, 1, device_id=device, device_id_type=MESH)

    load_r.wait()
    squares = jnp.zeros((TRAITS, BLOCK), F32)
    for g in range(4):
        x = rv[:, 1024 * g:1024 * g + 1024]
        rl[g] = stacked(x)
        for i in range(8):
            t = x[:, i * 128:i * 128 + 128]
            squares = squares + t * t
    for g in range(4):
        load_x[g].wait()
        v = dot(rl[g], xv[1024 * g:1024 * g + 1024, :])
        if g == 0:
            acc[...] = v
        else:
            acc[...] += v
    rxs0[:, 0:512] = acc[0:64, 0:512] + acc[64:128, 0:512]
    rxs0[:, 512:640] = squares
    rxl[...] = acc[0:64, 512:1024] + acc[64:128, 512:1024]
    pl.semaphore_wait(barrier, len(partners))
    rs0 = ppl_scatter(lambda to: rxs0.at[ds(8 * to, 8), :], rxr0)

    def gram(buf, pairs, first, last):
        for q in range(first, last):
            rows = [p for p, other in pairs if other == q]
            if q % 2 == 0 and rows and (rows[0], q + 1) in pairs:
                continue
            wide = 2 if q % 2 == 1 and (rows[0], q - 1) in pairs else 1
            left = q + 1 - wide
            v = dot_tn(xv[0:ROWS, rows[0] * 128:rows[-1] * 128 + 128], xv[0:ROWS, left * 128:q * 128 + 128])
            for w in range(wide):
                for p in rows:
                    if (p, left + w) in pairs:
                        buf[pairs.index((p, left + w))] = v[(p - rows[0]) * 128:(p - rows[0]) * 128 + 128, w * 128:w * 128 + 128]

    gram(gram_a, PAIRS[0], 1, 4)
    rs_a = ppl_scatter(lambda to: gram_a.at[:, ds(16 * to, 16), :], gr_a)
    gram(gram_b, PAIRS[1], 5, 8)
    rs_b = ppl_scatter(lambda to: gram_b.at[:, ds(16 * to, 16), :], gr_b)
    cross = dot_tn(xv[0:ROWS, 0:512], xv[0:ROWS, 512:1024])
    for i, (p, q) in enumerate(PAIRS[2]):
        gram_c[i] = cross[p * 128:p * 128 + 128, (q - 4) * 128:(q - 4) * 128 + 128]
    high, low = split(cross)
    gch[...] = high
    gcl[...] = low

    for c in load_small:
        c.wait()
    shrink = jnp.zeros((NB, BLOCK), F32)
    for component, factor in enumerate(FACTORS):
        shrink = shrink + jnp.where(a_ref[...] == component, F32(factor), F32(0.0))
    mine_rows = ds(8 * me, 8)
    e_mine = ev[mine_rows, :]
    for q in range(NB):
        col = slice(q * 128, q * 128 + 128)
        scale = shrink[q:q + 1, :]
        w_high, w_low = split(invv[q] * scale)
        wh[q] = w_high
        wl[q] = w_low
        noise = jnp.concatenate([nv[0, :, col], nv[1, :, col]], axis=0)
        jit[:, col] = dot_nt(noise, facv[q], HIGHEST) * scale

    def linear(beta):
        for q in range(NB):
            col = slice(q * 128, q * 128 + 128)
            lin[:, col] = jnp.dot(beta[:, col], ldv[q], precision=HIGHEST, preferred_element_type=F32)

    linear(e_mine)

    def received(rxs, rxr, copies):
        arrived(copies)
        total = rxs[mine_rows, :]
        for j in range(7):
            total = total + rxr[j]
        return total

    def spread_of(sums):
        return jnp.sqrt(jnp.sum(sums, axis=1, keepdims=True) / people)

    def base_of(total, first, spread, sweep):
        out = []
        for i in range(total.shape[1] // 128):
            q = first + i
            col = slice(q * 128, q * 128 + 128)
            rhs = total[:, i * 128:i * 128 + 128] + lin[:, col]
            out.append(dot3(rhs, wh[q], wl[q]) + spread * jit[8 * sweep:8 * sweep + 8, col])
        return out

    def coupling(gram_ref, gr, copies, pairs, ms, mr):
        arrived(copies)
        rows = ds(16 * me, 16)
        total = gram_ref[:, rows, :]
        for j in range(7):
            total = total + gr[j]
        for q in sorted({q for _, q in pairs}):
            at = [i for i, (_, other) in enumerate(pairs) if other == q]
            v = dot3(total[at[0]:at[-1] + 1].reshape(len(at) * 16, 128), wh[q], wl[q]).reshape(len(at), 16, 128)
            ms[at[0]:at[-1] + 1] = v
            mr[at[0]:at[-1] + 1, rows, :] = v
        return ppl_gather(ms, mr.at[:, rows, :])

    def unpack(copies, pairs, mr):
        arrived(copies)
        for i, (p, q) in enumerate(pairs):
            m_high, m_low = split(mr[i])
            mh[p, :, q * 128:q * 128 + 128] = m_high
            ml[p, :, q * 128:q * 128 + 128] = m_low

    def chain(base, first, last, before, sweep, halves):
        base = dict(zip(range(first, last), base))
        gathers = []
        for q in range(first, last):
            col = slice(q * 128, q * 128 + 128)
            new = base[q]
            mine[sweep, :, col] = new
            if q + 1 < last:
                high, low = split(new - before[:, col])
                both = dot(jnp.concatenate([high, low], axis=0), mh[q, :, (q + 1) * 128:last * 128])
                change = both[:8] + both[8:] + dot(high, ml[q, :, (q + 1) * 128:last * 128])
                for later in range(q + 1, last):
                    at = (later - q - 1) * 128
                    base[later] = base[later] - change[:, at:at + 128]
            if q + 1 in halves:
                span = pl.ds((q - 3) * 128, 512)
                everyone[sweep, mine_rows, span] = mine[sweep, :, span]
                gathers.append(ppl_gather(mine.at[sweep, :, span], everyone.at[sweep, mine_rows, span]))
        return gathers

    def changes(gather, sweep, half):
        arrived(gather)
        col = slice(half * 512, half * 512 + 512)
        before = ev[:, col] if sweep == 0 else everyone[0, :, col]
        both = stacked(everyone[sweep, :, col] - before)
        chl[sweep, half] = both
        return both

    def half_delta(sweep):
        @pl.loop(0, 4)
        def _(g):
            v = dot_nt(chl[sweep, 0], xv[ds(g * 1024, 1024), 0:512])
            for i in range(8):
                col = slice(i * 128, i * 128 + 128)
                d[sweep, g * 8 + i] = v[0:64, col] + v[64:128, col]

    def reduce_residual(sweep, own_residual, between):
        order = [4, 3, 5, 2, 6, 1, 7]
        theirs = (1 - cc) * 16
        own = cc * 16
        core_slot, y_slot, z_slot = slots(2), slots(8), slots(7)

        def finish(group):
            v = dot_nt(chl[sweep, 1], xv[ds(group * 1024, 1024), 512:1024])
            for i in range(8):
                col = slice(i * 128, i * 128 + 128)
                d[sweep, group * 8 + i] += v[0:64, col] + v[64:128, col]

        core = []
        for i, y in enumerate((1 - yl, yl)):
            finish((1 - cc) * 2 + y)
            core.append(start(d.at[sweep, ds(theirs + 8 * y, 8)], cr.at[sweep, i], core_slot + i, on_core))
        finish(cc * 2 + 1 - yl)
        finish(cc * 2 + yl)

        core[0].wait_recv()
        far = own + 8 * (1 - yl)
        near = own + 8 * yl
        to_y = {}
        for k in order + [0]:
            z = lax.rem(zz + k, 8)
            d[sweep, far + z] += cr[sweep, 0, z]
            to_y[k] = start(d.at[sweep, far + z], yr.at[sweep, k], y_slot + k, on_y)
        core[1].wait_recv()
        for i in range(8):
            d[sweep, near + i] += cr[sweep, 1, i]
        between()
        to_z = []
        for k in order:
            to_y[k].wait_recv()
            z = lax.rem(zz + k, 8)
            d[sweep, near + z] += yr[sweep, k]
            to_z.append(start(d.at[sweep, near + z], zr.at[sweep, k - 1], z_slot + k - 1, on_z(k)))
        to_y[0].wait_recv()
        total = d[sweep, near + zz] + yr[sweep, 0]
        for i, k in enumerate(order):
            to_z[i].wait_recv()
            total = total + zr[sweep, k - 1]
        rn[sweep, near + zz] = own_residual(near + zz) - total

        z_slot, y_slot, near_slot, far_slot = slots(7), slots(8), slots(8), slots(8)
        mine_at = rn.at[sweep, near + zz]
        from_z = {}
        for k in order:
            from_z[k] = start(mine_at, mine_at, z_slot + k - 1, on_z(k))
        from_y, from_core = {}, {}
        from_y[0] = start(mine_at, mine_at, y_slot, on_y)
        from_core[0] = start(mine_at, mine_at, near_slot, on_core)
        for k in (1, 7, 2, 6, 3, 5, 4):
            from_z[k].wait_recv()
            tile = rn.at[sweep, near + lax.rem(zz + 8 - k, 8)]
            from_y[k] = start(tile, tile, y_slot + k, on_y)
            from_core[k] = start(tile, tile, near_slot + k, on_core)
        yield near // 8
        last = {}
        for k in (0, 1, 7, 2, 6, 3, 5, 4):
            from_y[k].wait_recv()
            tile = rn.at[sweep, far + lax.rem(zz + 8 - k, 8)]
            last[k] = start(tile, tile, far_slot + k, on_core)
        yield far // 8
        arrived(from_core.values())
        yield (theirs + 8 * yl) // 8
        arrived(last.values())
        yield (theirs + 8 * (1 - yl)) // 8

    total = received(rxs0, rxr0, rs0)
    spread = spread_of(total[:, 512:640])
    base = base_of(total[:, 0:512], 0, spread, 0)
    ag_a = coupling(gram_a, gr_a, rs_a, PAIRS[0], ms_a, mr_a)
    ag_b = coupling(gram_b, gr_b, rs_b, PAIRS[1], ms_b, mr_b)
    unpack(ag_a, PAIRS[0], mr_a)
    gather, = chain(base, 0, 4, e_mine, 0, (4,))
    both = changes(gather, 0, 0)
    v = dot(both, gch[...])
    rxs1[...] = rxl[...] - (v[0:64] + v[64:128] + dot(both[0:64], gcl[...]))
    rs1 = ppl_scatter(lambda to: rxs1.at[ds(8 * to, 8), :], rxr1)
    rs_c = ppl_scatter(lambda to: gram_c.at[:, ds(16 * to, 16), :], gr_c)
    half_delta(0)
    total = received(rxs1, rxr1, rs1)
    base = base_of(total, 4, spread, 0)
    unpack(ag_b, PAIRS[1], mr_b)
    gather, = chain(base, 4, 8, e_mine, 0, (8,))
    changes(gather, 0, 1)

    ag_c = []

    def cross_coupling():
        ag_c.extend(coupling(gram_c, gr_c, rs_c, PAIRS[2], ms_c, mr_c))
        linear(mine[0])

    def first_residual(tile):
        return rv[:, ds(tile * 128, 128)]

    squares = jnp.zeros((TRAITS, BLOCK), F32)
    for step, group in enumerate(reduce_residual(0, first_residual, cross_coupling)):
        tiles = [rn[0, group * 8 + i] for i in range(8)]
        for t in tiles:
            squares = squares + t * t
        v = dot(stacked(jnp.concatenate(tiles, axis=1)), xv[ds(group * 1024, 1024), :])
        if step == 0:
            acc[...] = v
        else:
            acc[...] += v
    rxs2[:, 0:1024] = acc[0:64, :] + acc[64:128, :]
    rxs2[:, 1024:1152] = squares
    rs2 = ppl_scatter(lambda to: rxs2.at[ds(8 * to, 8), :], rxr2)
    unpack(ag_c, PAIRS[2], mr_c)

    total = received(rxs2, rxr2, rs2)
    base = base_of(total[:, 0:1024], 0, spread_of(total[:, 1024:1152]), 1)
    gathers = chain(base, 0, 8, mine[0], 1, (4, 8))
    changes(gathers[0], 1, 0)
    half_delta(1)
    changes(gathers[1], 1, 1)
    e_out[...] = everyone[1]
    for group in reduce_residual(1, lambda tile: rn[0, tile], lambda: None):
        pass
    for i in range(ROWS // 128):
        r_out[:, i * 128:i * 128 + 128] = rn[1, i]
    for c in sends:
        c.wait_send()


def shards(people, genotypes, residual, effects, assignments, ld_blocks, ld_inverses, ld_factors, normals):
    hbm = pl.BlockSpec(memory_space=pl.ANY)
    vmem = pl.BlockSpec(memory_space=pltpu.VMEM)
    wide = (NB, BLOCK, BLOCK)
    scratch = [
        ((4096, SNPS), BF16), ((TRAITS, 4096), F32), ((TRAITS, SNPS), F32), (wide, F32), (wide, F32), (wide, F32),
        ((2, 8, SNPS), F32),
        ((4, 128, 1024), BF16), ((128, 1024), F32),
        ((TRAITS, 640), F32), ((TRAITS, 512), F32), ((TRAITS, 1152), F32),
        ((7, 8, 640), F32), ((7, 8, 512), F32), ((7, 8, 1152), F32), ((TRAITS, 512), F32),
    ]
    scratch += [((len(p), BLOCK, BLOCK), F32) for p in PAIRS]
    scratch += [((7, len(p), 16, BLOCK), F32) for p in PAIRS]
    scratch += [((len(p), 16, BLOCK), F32) for p in PAIRS]
    scratch += [((len(p), BLOCK, BLOCK), F32) for p in PAIRS]
    scratch += [
        ((512, 512), BF16), ((512, 512), BF16), ((NB, BLOCK, SNPS), BF16), ((NB, BLOCK, SNPS), BF16),
        (wide, BF16), (wide, BF16), ((16, SNPS), F32), ((8, SNPS), F32),
        ((2, 8, SNPS), F32), ((2, TRAITS, SNPS), F32), ((2, 2, 128, 512), BF16),
        ((2, TILES, TRAITS, 128), F32), ((2, 2, 8, TRAITS, 128), F32), ((2, 8, TRAITS, 128), F32),
        ((2, 7, TRAITS, 128), F32), ((2, TILES, TRAITS, 128), F32),
    ]
    slots = 3 * 7 + 3 * 7 + 3 * 7 + 4 * 7 + 2 * (2 + 8 + 7 + 7 + 8 + 8 + 8)
    return pl.pallas_call(
        functools.partial(kernel, people),
        out_shape=(
            jax.ShapeDtypeStruct(effects.shape, F32),
            jax.ShapeDtypeStruct(residual.shape, F32),
        ),
        in_specs=[hbm, hbm, hbm, vmem, hbm, hbm, hbm, hbm],
        out_specs=(vmem, vmem),
        scratch_shapes=[pltpu.VMEM(shape, dtype) for shape, dtype in scratch]
        + [pltpu.SemaphoreType.DMA((slots,)), pltpu.SemaphoreType.DMA((slots,)), pltpu.SemaphoreType.DMA((10,))],
        compiler_params=pltpu.CompilerParams(collective_id=0, has_side_effects=True, vmem_limit_bytes=58 << 20),
        cost_estimate=pl.CostEstimate(flops=20_000_000_000, bytes_accessed=16_000_000, transcendentals=0),
        name="gibbs_sweeps",
    )(genotypes, residual, effects, assignments.reshape(NB, BLOCK), ld_blocks, ld_inverses, ld_factors, normals)


def solution(mesh):
    people = ROWS * mesh.shape["ppl"]
    in_specs = (
        P("ppl", "snp"),
        P(None, "ppl"),
        P(None, "snp"),
        P("snp"),
        P("snp", None, None),
        P("snp", None, None),
        P("snp", None, None),
        P(None, None, "snp"),
    )
    out_specs = (P(None, "snp"), P(None, "ppl"))
    return jax.shard_map(
        functools.partial(shards, people), mesh=mesh, in_specs=in_specs, out_specs=out_specs, check_vma=False
    )
```

```python
import functools

import jax
import jax.numpy as jnp
from jax import lax
from jax.experimental import pallas as pl
from jax.experimental.pallas import tpu as pltpu
from jax.sharding import PartitionSpec as P

F32 = jnp.float32
BF16 = jnp.bfloat16
MESH = pl.DeviceIdType.MESH
HIGHEST = lax.Precision.HIGHEST
FACTORS = (0.0, 0.3, 0.6, 1.0)
TRAITS, ROWS, SNPS, BLOCK, NB = 64, 3840, 1024, 128, 8
TILES = 32
FAR_FIRST = (6, 2, 5, 7, 4, 1, 3)
PAIRS = (
    [(p, q) for q in range(1, 4) for p in range(q)],
    [(p, q) for q in range(5, 8) for p in range(4, q)],
    [(p, q) for q in range(4, 8) for p in range(4)],
)


def ds(start, size):
    return pl.ds(pl.multiple_of(start, size), size)


def dot(a, b):
    return jnp.dot(a, b, preferred_element_type=F32)


def dot_nt(a, b, precision=None):
    return lax.dot_general(a, b, (((1,), (1,)), ((), ())), precision=precision, preferred_element_type=F32)


def dot_tn(a, b):
    return lax.dot_general(a, b, (((0,), (0,)), ((), ())), preferred_element_type=F32)


def split(x):
    high = x.astype(BF16)
    return high, (x - high.astype(F32)).astype(BF16)


def stacked(x):
    return jnp.concatenate(split(x), axis=0)


def dot3(a, b_high, b_low):
    n = a.shape[0]
    high, low = split(a)
    both = dot(jnp.concatenate([high, low], axis=0), b_high)
    return both[:n] + both[n:] + dot(high, b_low)


def kernel(
    people,
    x_hbm, r_hbm, e_hbm, a_ref, ld_hbm, inv_hbm, fac_hbm, n_hbm,
    e_out, r_out,
    xv, rv, ev, ldv, invv, facv, nv,
    rl, acc, rxs0, rxs1, rxs2, rxr0, rxr1, rxr2, rxl,
    gram_a, gram_b, gram_c, gr_a, gr_b, gr_c, gy_c, gs_c, ms_a, ms_b, ms_c, mr_a, mr_b, mr_c, gch, gcl, mh, ml, wh, wl, jit, lin,
    mine, everyone, chl, d, cr, yr, zr, rn,
    send_sem, recv_sem, local_sem,
):
    me = lax.axis_index("ppl")
    snp = lax.axis_index("snp")
    yh, xx = me // 4, lax.rem(me, 4)
    yl, zz, cc = snp // 16, lax.rem(snp // 2, 8), lax.rem(snp, 2)

    def on_ppl(j):
        return {"ppl": lax.rem(yh + j // 4, 2) * 4 + lax.rem(xx + j % 4, 4), "snp": snp}

    def on_z(j):
        return {"ppl": me, "snp": yl * 16 + lax.rem(zz + j, 8) * 2 + cc}

    on_y = {"ppl": me, "snp": (1 - yl) * 16 + zz * 2 + cc}
    on_core = {"ppl": me, "snp": yl * 16 + zz * 2 + 1 - cc}

    sends = []
    count = [0]

    def slots(n):
        first = count[0]
        count[0] += n
        return first

    def copy(src, dst, slot, device):
        return pltpu.make_async_remote_copy(
            src_ref=src, dst_ref=dst, send_sem=send_sem.at[slot], recv_sem=recv_sem.at[slot],
            device_id=device, device_id_type=MESH,
        )

    def start(src, dst, slot, device):
        c = copy(src, dst, slot, device)
        c.start()
        sends.append(c)
        return c

    def ppl_scatter(src_of, dst):
        base = slots(7)
        return [start(src_of(on_ppl(j)["ppl"]), dst.at[j - 1], base + j - 1, on_ppl(j)) for j in FAR_FIRST]

    def ppl_gather(src, dst):
        base = slots(7)
        return [start(src, dst, base + j - 1, on_ppl(j)) for j in FAR_FIRST]

    def arrived(copies):
        for c in copies:
            c.wait_recv()

    def load(i, src, dst):
        c = pltpu.make_async_copy(src, dst, local_sem.at[i])
        c.start()
        return c

    load_r = load(0, r_hbm, rv.at[:, 0:ROWS])
    load_x = []
    for g in range(4):
        top = min(1024 * g + 1024, ROWS)
        part = pl.ds(1024 * g, top - 1024 * g)
        load_x.append(load(1 + g, x_hbm.at[part, :], xv.at[part, :]))
    load_small = [
        load(5, inv_hbm, invv), load(6, fac_hbm, facv), load(7, n_hbm.at[:, ds(8 * me, 8), :], nv),
        load(8, ld_hbm, ldv), load(9, e_hbm, ev),
    ]
    xv[ROWS:4096, :] = jnp.zeros((4096 - ROWS, SNPS), BF16)
    rv[:, ROWS:4096] = jnp.zeros((TRAITS, 4096 - ROWS), F32)

    barrier = pltpu.get_barrier_semaphore()
    partners = [on_ppl(j) for j in range(1, 8)] + [on_z(j) for j in range(1, 8)] + [on_y, on_core]
    for device in partners:
        pl.semaphore_signal(barrier, 1, device_id=device, device_id_type=MESH)

    load_r.wait()
    squares = jnp.zeros((TRAITS, BLOCK), F32)
    for g in range(4):
        x = rv[:, 1024 * g:1024 * g + 1024]
        rl[g] = stacked(x)
        for i in range(8):
            t = x[:, i * 128:i * 128 + 128]
            squares = squares + t * t
    for g in range(4):
        load_x[g].wait()
        v = dot(rl[g], xv[1024 * g:1024 * g + 1024, :])
        if g == 0:
            acc[...] = v
        else:
            acc[...] += v
    rxs0[:, 0:512] = acc[0:64, 0:512] + acc[64:128, 0:512]
    rxs0[:, 512:640] = squares
    rxl[...] = acc[0:64, 512:1024] + acc[64:128, 512:1024]

    def gram(buf, pairs, first, last):
        for q in range(first, last):
            rows = [p for p, other in pairs if other == q]
            if q % 2 == 0 and rows and (rows[0], q + 1) in pairs:
                continue
            wide = 2 if q % 2 == 1 and (rows[0], q - 1) in pairs else 1
            left = q + 1 - wide
            v = dot_tn(xv[0:ROWS, rows[0] * 128:rows[-1] * 128 + 128], xv[0:ROWS, left * 128:q * 128 + 128])
            for w in range(wide):
                for p in rows:
                    if (p, left + w) in pairs:
                        buf[pairs.index((p, left + w))] = v[(p - rows[0]) * 128:(p - rows[0]) * 128 + 128, w * 128:w * 128 + 128]

    gram(gram_a, PAIRS[0], 1, 4)
    gram(gram_b, PAIRS[1], 5, 8)

    for c in load_small:
        c.wait()
    shrink = jnp.zeros((NB, BLOCK), F32)
    for component, factor in enumerate(FACTORS):
        shrink = shrink + jnp.where(a_ref[...] == component, F32(factor), F32(0.0))
    mine_rows = ds(8 * me, 8)
    e_mine = ev[mine_rows, :]
    for q in range(NB):
        col = slice(q * 128, q * 128 + 128)
        scale = shrink[q:q + 1, :]
        w_high, w_low = split(invv[q] * scale)
        wh[q] = w_high
        wl[q] = w_low
        noise = jnp.concatenate([nv[0, :, col], nv[1, :, col]], axis=0)
        jit[:, col] = dot_nt(noise, facv[q], HIGHEST) * scale

    def linear(beta):
        for q in range(NB):
            col = slice(q * 128, q * 128 + 128)
            lin[:, col] = jnp.dot(beta[:, col], ldv[q], precision=HIGHEST, preferred_element_type=F32)

    linear(e_mine)

    pl.semaphore_wait(barrier, len(partners))
    rs0 = ppl_scatter(lambda to: rxs0.at[ds(8 * to, 8), :], rxr0)
    rs_a = ppl_scatter(lambda to: gram_a.at[:, ds(16 * to, 16), :], gr_a)
    cross = dot_tn(xv[0:ROWS, 0:512], xv[0:ROWS, 512:1024])
    for i, (p, q) in enumerate(PAIRS[2]):
        gram_c[i] = cross[p * 128:p * 128 + 128, (q - 4) * 128:(q - 4) * 128 + 128]
    high, low = split(cross)
    gch[...] = high
    gcl[...] = low

    def received(rxs, rxr, copies):
        arrived(copies)
        total = rxs[mine_rows, :]
        for j in range(7):
            total = total + rxr[j]
        return total

    def spread_of(sums):
        return jnp.sqrt(jnp.sum(sums, axis=1, keepdims=True) / people)

    def base_of(total, first, spread, sweep):
        out = []
        for i in range(total.shape[1] // 128):
            q = first + i
            col = slice(q * 128, q * 128 + 128)
            rhs = total[:, i * 128:i * 128 + 128] + lin[:, col]
            out.append(dot3(rhs, wh[q], wl[q]) + spread * jit[8 * sweep:8 * sweep + 8, col])
        return out

    def coupling(gram_ref, gr, copies, pairs, ms, mr):
        arrived(copies)
        rows = ds(16 * me, 16)
        total = gram_ref[:, rows, :]
        for j in range(7):
            total = total + gr[j]
        for q in sorted({q for _, q in pairs}):
            at = [i for i, (_, other) in enumerate(pairs) if other == q]
            v = dot3(total[at[0]:at[-1] + 1].reshape(len(at) * 16, 128), wh[q], wl[q]).reshape(len(at), 16, 128)
            ms[at[0]:at[-1] + 1] = v
            mr[at[0]:at[-1] + 1, rows, :] = v
        return ppl_gather(ms, mr.at[:, rows, :])

    def unpack(copies, pairs, mr):
        arrived(copies)
        for i, (p, q) in enumerate(pairs):
            m_high, m_low = split(mr[i])
            mh[p, :, q * 128:q * 128 + 128] = m_high
            ml[p, :, q * 128:q * 128 + 128] = m_low

    def chain(base, first, last, before, sweep):
        base = dict(zip(range(first, last), base))
        gathers = []
        for q in range(first, last):
            col = slice(q * 128, q * 128 + 128)
            new = base[q]
            mine[sweep, :, col] = new
            if q + 1 < last:
                high, low = split(new - before[:, col])
                both = dot(jnp.concatenate([high, low], axis=0), mh[q, :, (q + 1) * 128:last * 128])
                change = both[:8] + both[8:] + dot(high, ml[q, :, (q + 1) * 128:last * 128])
                for later in range(q + 1, last):
                    at = (later - q - 1) * 128
                    base[later] = base[later] - change[:, at:at + 128]
            if q % 4 == 3:
                span = pl.ds((q - 3) * 128, 512)
                everyone[sweep, mine_rows, span] = mine[sweep, :, span]
                gathers.append(ppl_gather(mine.at[sweep, :, span], everyone.at[sweep, mine_rows, span]))
        return gathers

    def changes(gather, sweep, half):
        arrived(gather)
        col = slice(half * 512, half * 512 + 512)
        before = ev[:, col] if sweep == 0 else everyone[0, :, col]
        both = stacked(everyone[sweep, :, col] - before)
        chl[sweep, half] = both
        return both

    def half_delta(sweep):
        @pl.loop(0, 4)
        def _(g):
            v = dot_nt(chl[sweep, 0], xv[ds(g * 1024, 1024), 0:512])
            for i in range(8):
                col = slice(i * 128, i * 128 + 128)
                d[sweep, g * 8 + i] = v[0:64, col] + v[64:128, col]

    def reduce_residual(sweep, own_residual, *between):
        far_first, near_first = (4, 3, 5, 2, 6, 1, 7, 0), (1, 7, 2, 6, 3, 5, 4)
        theirs = (1 - cc) * 16
        own = cc * 16
        far = own + 8 * (1 - yl)
        near = own + 8 * yl
        core_slot, y_slot, z_slot = slots(9), slots(8), slots(7)

        def finish(first):
            v = dot_nt(chl[sweep, 1], xv[ds(first * 128, 1024), 512:1024])
            for i in range(8):
                col = slice(i * 128, i * 128 + 128)
                d[sweep, first + i] += v[0:64, col] + v[64:128, col]

        finish(theirs + 8 * (1 - yl))
        core, to_y, to_z = {}, {}, {}
        for k in far_first:
            z = lax.rem(zz + k, 8)
            core[k] = start(d.at[sweep, theirs + 8 * (1 - yl) + z], cr.at[sweep, 0, k], core_slot + k, on_core)
        finish(far)
        for k in far_first:
            z = lax.rem(zz + k, 8)
            core[k].wait_recv()
            d[sweep, far + z] += cr[sweep, 0, k]
            to_y[k] = start(d.at[sweep, far + z], yr.at[sweep, k], y_slot + k, on_y)
        finish(theirs + 8 * yl)
        second = start(d.at[sweep, ds(theirs + 8 * yl, 8)], cr.at[sweep, 1], core_slot + 8, on_core)
        finish(near)
        second.wait_recv()
        for i in range(8):
            d[sweep, near + i] += cr[sweep, 1, i]
        for k in far_first[:7]:
            to_y[k].wait_recv()
            z = lax.rem(zz + k, 8)
            d[sweep, near + z] += yr[sweep, k]
            to_z[k] = start(d.at[sweep, near + z], zr.at[sweep, k - 1], z_slot + k - 1, on_z(k))
        to_y[0].wait_recv()
        total = d[sweep, near + zz] + yr[sweep, 0]
        for k in far_first[:7]:
            to_z[k].wait_recv()
            total = total + zr[sweep, k - 1]
        rn[sweep, near + zz] = own_residual(near + zz) - total

        z_slot, y_slot, near_slot, far_slot = slots(7), slots(8), slots(8), slots(8)
        mine_at = rn.at[sweep, near + zz]
        from_z, from_y, from_core, last = {}, {}, {}, {}
        from_y[0] = start(mine_at, mine_at, y_slot, on_y)
        for k in near_first:
            from_z[k] = start(mine_at, mine_at, z_slot + k - 1, on_z(k))
        from_core[0] = start(mine_at, mine_at, near_slot, on_core)
        if between:
            between[0]()
        for k in near_first:
            from_z[k].wait_recv()
            tile = rn.at[sweep, near + lax.rem(zz + 8 - k, 8)]
            from_y[k] = start(tile, tile, y_slot + k, on_y)
            from_core[k] = start(tile, tile, near_slot + k, on_core)
        if between:
            between[1]()
        yield near // 8
        for k in (0,) + near_first:
            from_y[k].wait_recv()
            tile = rn.at[sweep, far + lax.rem(zz + 8 - k, 8)]
            last[k] = start(tile, tile, far_slot + k, on_core)
        yield far // 8
        arrived(from_core.values())
        yield (theirs + 8 * yl) // 8
        arrived(last.values())
        yield (theirs + 8 * (1 - yl)) // 8

    total = received(rxs0, rxr0, rs0)
    spread = spread_of(total[:, 512:640])
    base = base_of(total[:, 0:512], 0, spread, 0)
    ag_a = coupling(gram_a, gr_a, rs_a, PAIRS[0], ms_a, mr_a)
    rs_b = ppl_scatter(lambda to: gram_b.at[:, ds(16 * to, 16), :], gr_b)
    unpack(ag_a, PAIRS[0], mr_a)
    gather, = chain(base, 0, 4, e_mine, 0)
    both = changes(gather, 0, 0)
    v = dot(both, gch[...])
    rxs1[...] = rxl[...] - (v[0:64] + v[64:128] + dot(both[0:64], gcl[...]))
    rs1 = ppl_scatter(lambda to: rxs1.at[ds(8 * to, 8), :], rxr1)
    ag_b = coupling(gram_b, gr_b, rs_b, PAIRS[1], ms_b, mr_b)
    half_delta(0)
    total = received(rxs1, rxr1, rs1)
    base = base_of(total, 4, spread, 0)
    unpack(ag_b, PAIRS[1], mr_b)
    gather, = chain(base, 4, 8, e_mine, 0)
    changes(gather, 0, 1)

    rows = ds(32 * xx, 32)
    pending = {}

    def on_x(j):
        return {"ppl": yh * 4 + lax.rem(xx + j, 4), "snp": snp}

    def cross_scatter():
        base = slots(3)
        pending["x"] = [
            start(gram_c.at[:, ds(32 * lax.rem(xx + j, 4), 32), :], gr_c.at[j - 1], base + j - 1, on_x(j)) for j in (2, 1, 3)
        ]

    def cross_sum():
        arrived(pending["x"])
        gs_c[...] = gram_c[:, rows, :] + gr_c[0] + gr_c[1] + gr_c[2]
        pending["y"] = [start(gs_c, gy_c, slots(1), on_ppl(4))]

    def cross_coupling():
        arrived(pending["y"])
        for q in range(4, 8):
            at = slice((q - 4) * 4, (q - 4) * 4 + 4)
            v = dot3((gs_c[at] + gy_c[at]).reshape(128, 128), wh[q], wl[q]).reshape(4, 32, 128)
            ms_c[at] = v
            mr_c[at, rows, :] = v
        base = slots(3)
        pending["m"] = [start(ms_c, mr_c.at[:, rows, :], base + j - 1, on_x(j)) for j in (2, 1, 3)]

    cross_scatter()
    squares = jnp.zeros((TRAITS, BLOCK), F32)
    for step, group in enumerate(reduce_residual(0, lambda tile: rv[:, ds(tile * 128, 128)], cross_sum, cross_coupling)):
        tiles = [rn[0, group * 8 + i] for i in range(8)]
        for t in tiles:
            squares = squares + t * t
        v = dot(stacked(jnp.concatenate(tiles, axis=1)), xv[ds(group * 1024, 1024), :])
        if step == 0:
            acc[...] = v
        else:
            acc[...] += v
    rxs2[:, 0:1024] = acc[0:64, :] + acc[64:128, :]
    rxs2[:, 1024:1152] = squares
    rs2 = ppl_scatter(lambda to: rxs2.at[ds(8 * to, 8), :], rxr2)
    linear(mine[0])

    total = received(rxs2, rxr2, rs2)
    base = base_of(total[:, 0:1024], 0, spread_of(total[:, 1024:1152]), 1)
    first_gather, = chain(base[0:4], 0, 4, mine[0], 1)
    unpack(pending["m"], PAIRS[2], mr_c)
    high, low = split(mine[1, :, 0:512] - mine[0, :, 0:512])
    both = dot(jnp.concatenate([high, low], axis=0), mh[0:4, :, 512:1024].reshape(512, 512))
    change = both[:8] + both[8:] + dot(high, ml[0:4, :, 512:1024].reshape(512, 512))
    later = [base[4 + i] - change[:, i * 128:i * 128 + 128] for i in range(4)]
    second_gather, = chain(later, 4, 8, mine[0], 1)
    changes(first_gather, 1, 0)
    half_delta(1)
    changes(second_gather, 1, 1)
    e_out[...] = everyone[1]
    copies = []
    for group in reduce_residual(1, lambda tile: rn[0, tile]):
        for i in range(8):
            tile = group * 8 + i
            copies.append(pltpu.make_async_copy(rn.at[1, tile], r_out.at[:, ds(tile * 128, 128)], local_sem.at[len(copies)]))
            copies[-1].start()
    for c in copies:
        c.wait()
    for c in sends:
        c.wait_send()


def deliver(e_ref, r_ref, e_out, r_out):
    e_out[...] = e_ref[...]
    r_out[...] = r_ref[:, 0:ROWS]


def shards(people, genotypes, residual, effects, assignments, ld_blocks, ld_inverses, ld_factors, normals):
    hbm = pl.BlockSpec(memory_space=pl.ANY)
    vmem = pl.BlockSpec(memory_space=pltpu.VMEM)
    wide = (NB, BLOCK, BLOCK)
    scratch = [
        ((4096, SNPS), BF16), ((TRAITS, 4096), F32), ((TRAITS, SNPS), F32), (wide, F32), (wide, F32), (wide, F32),
        ((2, 8, SNPS), F32),
        ((4, 128, 1024), BF16), ((128, 1024), F32),
        ((TRAITS, 640), F32), ((TRAITS, 512), F32), ((TRAITS, 1152), F32),
        ((7, 8, 640), F32), ((7, 8, 512), F32), ((7, 8, 1152), F32), ((TRAITS, 512), F32),
    ]
    scratch += [((len(p), BLOCK, BLOCK), F32) for p in PAIRS]
    cross = (len(PAIRS[2]), 32, BLOCK)
    scratch += [((7, len(p), 16, BLOCK), F32) for p in PAIRS[:2]] + [((3, *cross), F32), (cross, F32), (cross, F32)]
    scratch += [((len(p), 16, BLOCK), F32) for p in PAIRS[:2]] + [(cross, F32)]
    scratch += [((len(p), BLOCK, BLOCK), F32) for p in PAIRS]
    scratch += [
        ((512, 512), BF16), ((512, 512), BF16), ((NB, BLOCK, SNPS), BF16), ((NB, BLOCK, SNPS), BF16),
        (wide, BF16), (wide, BF16), ((16, SNPS), F32), ((8, SNPS), F32),
        ((2, 8, SNPS), F32), ((2, TRAITS, SNPS), F32), ((2, 2, 128, 512), BF16),
        ((2, TILES, TRAITS, 128), F32), ((2, 2, 8, TRAITS, 128), F32), ((2, 8, TRAITS, 128), F32),
        ((2, 7, TRAITS, 128), F32), ((2, TILES, TRAITS, 128), F32),
    ]
    slots = 3 * 7 + 2 * 7 + 2 * 7 + 7 + 4 * 7 + 2 * (9 + 8 + 7 + 7 + 8 + 8 + 8)
    e_new, r_new = pl.pallas_call(
        functools.partial(kernel, people),
        out_shape=(
            jax.ShapeDtypeStruct(effects.shape, F32),
            jax.ShapeDtypeStruct((TRAITS, TILES * 128), F32),
        ),
        in_specs=[hbm, hbm, hbm, vmem, hbm, hbm, hbm, hbm],
        out_specs=(vmem, hbm),
        scratch_shapes=[pltpu.VMEM(shape, dtype) for shape, dtype in scratch]
        + [pltpu.SemaphoreType.DMA((slots,)), pltpu.SemaphoreType.DMA((slots,)), pltpu.SemaphoreType.DMA((33,))],
        compiler_params=pltpu.CompilerParams(collective_id=0, has_side_effects=True, vmem_limit_bytes=58 << 20),
        cost_estimate=pl.CostEstimate(flops=20_000_000_000, bytes_accessed=16_000_000, transcendentals=0),
        name="gibbs_sweeps",
    )(genotypes, residual, effects, assignments.reshape(NB, BLOCK), ld_blocks, ld_inverses, ld_factors, normals)
    return pl.pallas_call(
        deliver,
        out_shape=(jax.ShapeDtypeStruct(effects.shape, F32), jax.ShapeDtypeStruct(residual.shape, F32)),
        in_specs=[vmem, vmem],
        out_specs=(vmem, vmem),
        name="deliver",
    )(e_new, r_new)


def solution(mesh):
    people = ROWS * mesh.shape["ppl"]
    in_specs = (
        P("ppl", "snp"),
        P(None, "ppl"),
        P(None, "snp"),
        P("snp"),
        P("snp", None, None),
        P("snp", None, None),
        P("snp", None, None),
        P(None, None, "snp"),
    )
    out_specs = (P(None, "snp"), P(None, "ppl"))
    return jax.shard_map(
        functools.partial(shards, people), mesh=mesh, in_specs=in_specs, out_specs=out_specs, check_vma=False
    )
```

```python
import functools

import jax
import jax.numpy as jnp
from jax import lax
from jax.experimental import pallas as pl
from jax.experimental.pallas import tpu as pltpu
from jax.sharding import PartitionSpec as P

F32 = jnp.float32
BF16 = jnp.bfloat16
MESH = pl.DeviceIdType.MESH
HIGHEST = lax.Precision.HIGHEST
FACTORS = (0.0, 0.3, 0.6, 1.0)
TRAITS, ROWS, SNPS, BLOCK, NB = 64, 3840, 1024, 128, 8
TILES = 32
FAR_FIRST = (6, 2, 5, 7, 4, 1, 3)
PAIRS = (
    [(p, q) for q in range(1, 4) for p in range(q)],
    [(p, q) for q in range(5, 8) for p in range(4, q)],
    [(p, q) for q in range(4, 8) for p in range(4)],
)


def ds(start, size):
    return pl.ds(pl.multiple_of(start, size), size)


def dot(a, b):
    return jnp.dot(a, b, preferred_element_type=F32)


def dot_nt(a, b, precision=None):
    return lax.dot_general(a, b, (((1,), (1,)), ((), ())), precision=precision, preferred_element_type=F32)


def dot_tn(a, b):
    return lax.dot_general(a, b, (((0,), (0,)), ((), ())), preferred_element_type=F32)


def split(x):
    high = x.astype(BF16)
    return high, (x - high.astype(F32)).astype(BF16)


def stacked(x):
    return jnp.concatenate(split(x), axis=0)


def dot3(a, b_high, b_low):
    n = a.shape[0]
    high, low = split(a)
    both = dot(jnp.concatenate([high, low], axis=0), b_high)
    return both[:n] + both[n:] + dot(high, b_low)


def kernel(
    people,
    x_hbm, r_hbm, e_hbm, a_ref, ld_hbm, inv_hbm, fac_hbm, n_hbm,
    e_out, r_out,
    xv, rv, ev, ldv, invv, facv, nv,
    rl, acc, rxs0, rxs1, rxs2, rxr0, rxr1, rxr2, rxl,
    gram_a, gram_b, gram_c, gr_a, gr_b, gr_c, gy_c, gs_c, ms_a, ms_b, ms_c, mr_a, mr_b, mr_c, gch, gcl, mh, ml, wh, wl, jit, lin,
    mine, everyone, chl, d, cr, yr, zr, rn,
    send_sem, recv_sem, local_sem,
):
    me = lax.axis_index("ppl")
    snp = lax.axis_index("snp")
    yh, xx = me // 4, lax.rem(me, 4)
    yl, zz, cc = snp // 16, lax.rem(snp // 2, 8), lax.rem(snp, 2)

    def on_ppl(j):
        return {"ppl": lax.rem(yh + j // 4, 2) * 4 + lax.rem(xx + j % 4, 4), "snp": snp}

    def on_z(j):
        return {"ppl": me, "snp": yl * 16 + lax.rem(zz + j, 8) * 2 + cc}

    on_y = {"ppl": me, "snp": (1 - yl) * 16 + zz * 2 + cc}
    on_core = {"ppl": me, "snp": yl * 16 + zz * 2 + 1 - cc}

    sends = []
    count = [0]

    def slots(n):
        first = count[0]
        count[0] += n
        return first

    def copy(src, dst, slot, device):
        return pltpu.make_async_remote_copy(
            src_ref=src, dst_ref=dst, send_sem=send_sem.at[slot], recv_sem=recv_sem.at[slot],
            device_id=device, device_id_type=MESH,
        )

    def start(src, dst, slot, device):
        c = copy(src, dst, slot, device)
        c.start()
        sends.append(c)
        return c

    def ppl_scatter(src_of, dst):
        base = slots(7)
        return [start(src_of(on_ppl(j)["ppl"]), dst.at[j - 1], base + j - 1, on_ppl(j)) for j in FAR_FIRST]

    def ppl_gather(src, dst):
        base = slots(7)
        return [start(src, dst, base + j - 1, on_ppl(j)) for j in FAR_FIRST]

    def arrived(copies):
        for c in copies:
            c.wait_recv()

    def load(i, src, dst):
        c = pltpu.make_async_copy(src, dst, local_sem.at[i])
        c.start()
        return c

    load_r = load(0, r_hbm, rv.at[:, 0:ROWS])
    load_x = []
    for g in range(4):
        top = min(1024 * g + 1024, ROWS)
        part = pl.ds(1024 * g, top - 1024 * g)
        load_x.append(load(1 + g, x_hbm.at[part, :], xv.at[part, :]))
    load_small = [
        load(5, inv_hbm, invv), load(6, fac_hbm, facv), load(7, n_hbm.at[:, ds(8 * me, 8), :], nv),
        load(8, ld_hbm, ldv), load(9, e_hbm, ev),
    ]
    xv[ROWS:4096, :] = jnp.zeros((4096 - ROWS, SNPS), BF16)
    rv[:, ROWS:4096] = jnp.zeros((TRAITS, 4096 - ROWS), F32)

    barrier = pltpu.get_barrier_semaphore()
    partners = [on_ppl(j) for j in range(1, 8)] + [on_z(j) for j in range(1, 8)] + [on_y, on_core]
    for device in partners:
        pl.semaphore_signal(barrier, 1, device_id=device, device_id_type=MESH)

    load_r.wait()
    squares = jnp.zeros((TRAITS, BLOCK), F32)
    for g in range(4):
        x = rv[:, 1024 * g:1024 * g + 1024]
        rl[g] = stacked(x)
        for i in range(8):
            t = x[:, i * 128:i * 128 + 128]
            squares = squares + t * t
    for g in range(4):
        load_x[g].wait()
        v = dot(rl[g], xv[1024 * g:1024 * g + 1024, :])
        if g == 0:
            acc[...] = v
        else:
            acc[...] += v
    rxs0[:, 0:512] = acc[0:64, 0:512] + acc[64:128, 0:512]
    rxs0[:, 512:640] = squares
    rxl[...] = acc[0:64, 512:1024] + acc[64:128, 512:1024]

    def gram(buf, pairs, first, last):
        for q in range(first, last):
            rows = [p for p, other in pairs if other == q]
            if q % 2 == 0 and rows and (rows[0], q + 1) in pairs:
                continue
            wide = 2 if q % 2 == 1 and (rows[0], q - 1) in pairs else 1
            left = q + 1 - wide
            v = dot_tn(xv[0:ROWS, rows[0] * 128:rows[-1] * 128 + 128], xv[0:ROWS, left * 128:q * 128 + 128])
            for w in range(wide):
                for p in rows:
                    if (p, left + w) in pairs:
                        buf[pairs.index((p, left + w))] = v[(p - rows[0]) * 128:(p - rows[0]) * 128 + 128, w * 128:w * 128 + 128]

    gram(gram_a, PAIRS[0], 1, 4)
    pl.semaphore_wait(barrier, len(partners))
    rs0 = ppl_scatter(lambda to: rxs0.at[ds(8 * to, 8), :], rxr0)
    rs_a = ppl_scatter(lambda to: gram_a.at[:, ds(16 * to, 16), :], gr_a)

    for c in load_small:
        c.wait()
    shrink = jnp.zeros((NB, BLOCK), F32)
    for component, factor in enumerate(FACTORS):
        shrink = shrink + jnp.where(a_ref[...] == component, F32(factor), F32(0.0))
    mine_rows = ds(8 * me, 8)
    e_mine = ev[mine_rows, :]
    for q in range(NB):
        col = slice(q * 128, q * 128 + 128)
        scale = shrink[q:q + 1, :]
        w_high, w_low = split(invv[q] * scale)
        wh[q] = w_high
        wl[q] = w_low
        noise = jnp.concatenate([nv[0, :, col], nv[1, :, col]], axis=0)
        jit[:, col] = dot_nt(noise, facv[q], HIGHEST) * scale

    def linear(beta):
        for q in range(NB):
            col = slice(q * 128, q * 128 + 128)
            lin[:, col] = jnp.dot(beta[:, col], ldv[q], precision=HIGHEST, preferred_element_type=F32)

    linear(e_mine)

    gram(gram_b, PAIRS[1], 5, 8)
    cross = dot_tn(xv[0:ROWS, 0:512], xv[0:ROWS, 512:1024])
    for i, (p, q) in enumerate(PAIRS[2]):
        gram_c[i] = cross[p * 128:p * 128 + 128, (q - 4) * 128:(q - 4) * 128 + 128]
    high, low = split(cross)
    gch[...] = high
    gcl[...] = low

    def received(rxs, rxr, copies):
        arrived(copies)
        total = rxs[mine_rows, :]
        for j in range(7):
            total = total + rxr[j]
        return total

    def spread_of(sums):
        return jnp.sqrt(jnp.sum(sums, axis=1, keepdims=True) / people)

    def base_of(total, first, spread, sweep):
        out = []
        for i in range(total.shape[1] // 128):
            q = first + i
            col = slice(q * 128, q * 128 + 128)
            rhs = total[:, i * 128:i * 128 + 128] + lin[:, col]
            out.append(dot3(rhs, wh[q], wl[q]) + spread * jit[8 * sweep:8 * sweep + 8, col])
        return out

    def coupling(gram_ref, gr, copies, pairs, ms, mr):
        arrived(copies)
        rows = ds(16 * me, 16)
        total = gram_ref[:, rows, :]
        for j in range(7):
            total = total + gr[j]
        for q in sorted({q for _, q in pairs}):
            at = [i for i, (_, other) in enumerate(pairs) if other == q]
            v = dot3(total[at[0]:at[-1] + 1].reshape(len(at) * 16, 128), wh[q], wl[q]).reshape(len(at), 16, 128)
            ms[at[0]:at[-1] + 1] = v
            mr[at[0]:at[-1] + 1, rows, :] = v
        return ppl_gather(ms, mr.at[:, rows, :])

    def unpack(copies, pairs, mr):
        arrived(copies)
        for i, (p, q) in enumerate(pairs):
            m_high, m_low = split(mr[i])
            mh[p, :, q * 128:q * 128 + 128] = m_high
            ml[p, :, q * 128:q * 128 + 128] = m_low

    def chain(base, first, last, before, sweep):
        base = dict(zip(range(first, last), base))
        gathers = []
        for q in range(first, last):
            col = slice(q * 128, q * 128 + 128)
            new = base[q]
            mine[sweep, :, col] = new
            if q + 1 < last:
                high, low = split(new - before[:, col])
                both = dot(jnp.concatenate([high, low], axis=0), mh[q, :, (q + 1) * 128:last * 128])
                change = both[:8] + both[8:] + dot(high, ml[q, :, (q + 1) * 128:last * 128])
                for later in range(q + 1, last):
                    at = (later - q - 1) * 128
                    base[later] = base[later] - change[:, at:at + 128]
            if q % 4 == 3:
                span = pl.ds((q - 3) * 128, 512)
                everyone[sweep, mine_rows, span] = mine[sweep, :, span]
                gathers.append(ppl_gather(mine.at[sweep, :, span], everyone.at[sweep, mine_rows, span]))
        return gathers

    def changes(gather, sweep, half):
        arrived(gather)
        col = slice(half * 512, half * 512 + 512)
        before = ev[:, col] if sweep == 0 else everyone[0, :, col]
        both = stacked(everyone[sweep, :, col] - before)
        chl[sweep, half] = both
        return both

    def half_delta(sweep):
        @pl.loop(0, 4)
        def _(g):
            v = dot_nt(chl[sweep, 0], xv[ds(g * 1024, 1024), 0:512])
            for i in range(8):
                col = slice(i * 128, i * 128 + 128)
                d[sweep, g * 8 + i] = v[0:64, col] + v[64:128, col]

    def reduce_residual(sweep, own_residual, *between):
        far_first, near_first = (4, 3, 5, 2, 6, 1, 7, 0), (1, 7, 2, 6, 3, 5, 4)
        theirs = (1 - cc) * 16
        own = cc * 16
        far = own + 8 * (1 - yl)
        near = own + 8 * yl
        core_slot, y_slot, z_slot = slots(9), slots(8), slots(7)

        def finish(first):
            v = dot_nt(chl[sweep, 1], xv[ds(first * 128, 1024), 512:1024])
            for i in range(8):
                col = slice(i * 128, i * 128 + 128)
                d[sweep, first + i] += v[0:64, col] + v[64:128, col]

        finish(theirs + 8 * (1 - yl))
        core, to_y, to_z = {}, {}, {}
        for k in far_first:
            z = lax.rem(zz + k, 8)
            core[k] = start(d.at[sweep, theirs + 8 * (1 - yl) + z], cr.at[sweep, 0, k], core_slot + k, on_core)
        finish(far)
        for k in far_first:
            z = lax.rem(zz + k, 8)
            core[k].wait_recv()
            d[sweep, far + z] += cr[sweep, 0, k]
            to_y[k] = start(d.at[sweep, far + z], yr.at[sweep, k], y_slot + k, on_y)
        finish(theirs + 8 * yl)
        second = start(d.at[sweep, ds(theirs + 8 * yl, 8)], cr.at[sweep, 1], core_slot + 8, on_core)
        finish(near)
        second.wait_recv()
        for i in range(8):
            d[sweep, near + i] += cr[sweep, 1, i]
        for k in far_first[:7]:
            to_y[k].wait_recv()
            z = lax.rem(zz + k, 8)
            d[sweep, near + z] += yr[sweep, k]
            to_z[k] = start(d.at[sweep, near + z], zr.at[sweep, k - 1], z_slot + k - 1, on_z(k))
        if between:
            between[0]()
        to_y[0].wait_recv()
        total = d[sweep, near + zz] + yr[sweep, 0]
        for k in far_first[:7]:
            to_z[k].wait_recv()
            total = total + zr[sweep, k - 1]
        rn[sweep, near + zz] = own_residual(near + zz) - total

        z_slot, y_slot, near_slot, far_slot = slots(7), slots(8), slots(8), slots(8)
        mine_at = rn.at[sweep, near + zz]
        from_z, from_y, from_core, last = {}, {}, {}, {}
        from_y[0] = start(mine_at, mine_at, y_slot, on_y)
        for k in near_first:
            from_z[k] = start(mine_at, mine_at, z_slot + k - 1, on_z(k))
        from_core[0] = start(mine_at, mine_at, near_slot, on_core)
        if between:
            between[1]()
        for k in near_first:
            from_z[k].wait_recv()
            tile = rn.at[sweep, near + lax.rem(zz + 8 - k, 8)]
            from_y[k] = start(tile, tile, y_slot + k, on_y)
            from_core[k] = start(tile, tile, near_slot + k, on_core)
        yield near // 8
        for k in (0,) + near_first:
            from_y[k].wait_recv()
            tile = rn.at[sweep, far + lax.rem(zz + 8 - k, 8)]
            last[k] = start(tile, tile, far_slot + k, on_core)
        yield far // 8
        arrived(from_core.values())
        yield (theirs + 8 * yl) // 8
        arrived(last.values())
        yield (theirs + 8 * (1 - yl)) // 8

    total = received(rxs0, rxr0, rs0)
    spread = spread_of(total[:, 512:640])
    base = base_of(total[:, 0:512], 0, spread, 0)
    ag_a = coupling(gram_a, gr_a, rs_a, PAIRS[0], ms_a, mr_a)
    rs_b = ppl_scatter(lambda to: gram_b.at[:, ds(16 * to, 16), :], gr_b)
    unpack(ag_a, PAIRS[0], mr_a)
    gather, = chain(base, 0, 4, e_mine, 0)
    both = changes(gather, 0, 0)
    v = dot(both, gch[...])
    rxs1[...] = rxl[...] - (v[0:64] + v[64:128] + dot(both[0:64], gcl[...]))
    rs1 = ppl_scatter(lambda to: rxs1.at[ds(8 * to, 8), :], rxr1)
    ag_b = coupling(gram_b, gr_b, rs_b, PAIRS[1], ms_b, mr_b)
    half_delta(0)
    total = received(rxs1, rxr1, rs1)
    base = base_of(total, 4, spread, 0)
    unpack(ag_b, PAIRS[1], mr_b)
    gather, = chain(base, 4, 8, e_mine, 0)

    rows = ds(32 * xx, 32)
    pending = {}

    def on_x(j):
        return {"ppl": yh * 4 + lax.rem(xx + j, 4), "snp": snp}

    def cross_scatter():
        base = slots(3)
        pending["x"] = [
            start(gram_c.at[:, ds(32 * lax.rem(xx + j, 4), 32), :], gr_c.at[j - 1], base + j - 1, on_x(j)) for j in (2, 1, 3)
        ]

    def cross_sum():
        arrived(pending["x"])
        gs_c[...] = gram_c[:, rows, :] + gr_c[0] + gr_c[1] + gr_c[2]
        pending["y"] = [start(gs_c, gy_c, slots(1), on_ppl(4))]

    def cross_coupling():
        arrived(pending["y"])
        for q in range(4, 8):
            at = slice((q - 4) * 4, (q - 4) * 4 + 4)
            v = dot3((gs_c[at] + gy_c[at]).reshape(128, 128), wh[q], wl[q]).reshape(4, 32, 128)
            ms_c[at] = v
            mr_c[at, rows, :] = v
        base = slots(3)
        pending["m"] = [start(ms_c, mr_c.at[:, rows, :], base + j - 1, on_x(j)) for j in (2, 1, 3)]

    cross_scatter()
    changes(gather, 0, 1)
    squares = jnp.zeros((TRAITS, BLOCK), F32)
    for step, group in enumerate(reduce_residual(0, lambda tile: rv[:, ds(tile * 128, 128)], cross_sum, cross_coupling)):
        tiles = [rn[0, group * 8 + i] for i in range(8)]
        for t in tiles:
            squares = squares + t * t
        v = dot(stacked(jnp.concatenate(tiles, axis=1)), xv[ds(group * 1024, 1024), :])
        if step == 0:
            acc[...] = v
        else:
            acc[...] += v
    rxs2[:, 0:1024] = acc[0:64, :] + acc[64:128, :]
    rxs2[:, 1024:1152] = squares
    rs2 = ppl_scatter(lambda to: rxs2.at[ds(8 * to, 8), :], rxr2)
    linear(mine[0])

    total = received(rxs2, rxr2, rs2)
    base = base_of(total[:, 0:1024], 0, spread_of(total[:, 1024:1152]), 1)
    first_gather, = chain(base[0:4], 0, 4, mine[0], 1)
    unpack(pending["m"], PAIRS[2], mr_c)
    high, low = split(mine[1, :, 0:512] - mine[0, :, 0:512])
    both = dot(jnp.concatenate([high, low], axis=0), mh[0:4, :, 512:1024].reshape(512, 512))
    change = both[:8] + both[8:] + dot(high, ml[0:4, :, 512:1024].reshape(512, 512))
    later = [base[4 + i] - change[:, i * 128:i * 128 + 128] for i in range(4)]
    second_gather, = chain(later, 4, 8, mine[0], 1)
    changes(first_gather, 1, 0)
    half_delta(1)
    changes(second_gather, 1, 1)
    e_out[...] = everyone[1]
    copies = []
    for group in reduce_residual(1, lambda tile: rn[0, tile]):
        for i in range(8):
            tile = group * 8 + i
            copies.append(pltpu.make_async_copy(rn.at[1, tile], r_out.at[:, ds(tile * 128, 128)], local_sem.at[len(copies)]))
            copies[-1].start()
    for c in copies:
        c.wait()
    for c in sends:
        c.wait_send()


def deliver(e_ref, r_ref, e_out, r_out):
    e_out[...] = e_ref[...]
    r_out[...] = r_ref[:, 0:ROWS]


def shards(people, genotypes, residual, effects, assignments, ld_blocks, ld_inverses, ld_factors, normals):
    hbm = pl.BlockSpec(memory_space=pl.ANY)
    vmem = pl.BlockSpec(memory_space=pltpu.VMEM)
    wide = (NB, BLOCK, BLOCK)
    scratch = [
        ((4096, SNPS), BF16), ((TRAITS, 4096), F32), ((TRAITS, SNPS), F32), (wide, F32), (wide, F32), (wide, F32),
        ((2, 8, SNPS), F32),
        ((4, 128, 1024), BF16), ((128, 1024), F32),
        ((TRAITS, 640), F32), ((TRAITS, 512), F32), ((TRAITS, 1152), F32),
        ((7, 8, 640), F32), ((7, 8, 512), F32), ((7, 8, 1152), F32), ((TRAITS, 512), F32),
    ]
    scratch += [((len(p), BLOCK, BLOCK), F32) for p in PAIRS]
    cross = (len(PAIRS[2]), 32, BLOCK)
    scratch += [((7, len(p), 16, BLOCK), F32) for p in PAIRS[:2]] + [((3, *cross), F32), (cross, F32), (cross, F32)]
    scratch += [((len(p), 16, BLOCK), F32) for p in PAIRS[:2]] + [(cross, F32)]
    scratch += [((len(p), BLOCK, BLOCK), F32) for p in PAIRS]
    scratch += [
        ((512, 512), BF16), ((512, 512), BF16), ((NB, BLOCK, SNPS), BF16), ((NB, BLOCK, SNPS), BF16),
        (wide, BF16), (wide, BF16), ((16, SNPS), F32), ((8, SNPS), F32),
        ((2, 8, SNPS), F32), ((2, TRAITS, SNPS), F32), ((2, 2, 128, 512), BF16),
        ((2, TILES, TRAITS, 128), F32), ((2, 2, 8, TRAITS, 128), F32), ((2, 8, TRAITS, 128), F32),
        ((2, 7, TRAITS, 128), F32), ((2, TILES, TRAITS, 128), F32),
    ]
    slots = 3 * 7 + 2 * 7 + 2 * 7 + 7 + 4 * 7 + 2 * (9 + 8 + 7 + 7 + 8 + 8 + 8)
    e_new, r_new = pl.pallas_call(
        functools.partial(kernel, people),
        out_shape=(
            jax.ShapeDtypeStruct(effects.shape, F32),
            jax.ShapeDtypeStruct((TRAITS, TILES * 128), F32),
        ),
        in_specs=[hbm, hbm, hbm, vmem, hbm, hbm, hbm, hbm],
        out_specs=(vmem, hbm),
        scratch_shapes=[pltpu.VMEM(shape, dtype) for shape, dtype in scratch]
        + [pltpu.SemaphoreType.DMA((slots,)), pltpu.SemaphoreType.DMA((slots,)), pltpu.SemaphoreType.DMA((33,))],
        compiler_params=pltpu.CompilerParams(collective_id=0, has_side_effects=True, vmem_limit_bytes=58 << 20),
        cost_estimate=pl.CostEstimate(flops=20_000_000_000, bytes_accessed=16_000_000, transcendentals=0),
        name="gibbs_sweeps",
    )(genotypes, residual, effects, assignments.reshape(NB, BLOCK), ld_blocks, ld_inverses, ld_factors, normals)
    return pl.pallas_call(
        deliver,
        out_shape=(jax.ShapeDtypeStruct(effects.shape, F32), jax.ShapeDtypeStruct(residual.shape, F32)),
        in_specs=[vmem, vmem],
        out_specs=(vmem, vmem),
        name="deliver",
    )(e_new, r_new)


def solution(mesh):
    people = ROWS * mesh.shape["ppl"]
    in_specs = (
        P("ppl", "snp"),
        P(None, "ppl"),
        P(None, "snp"),
        P("snp"),
        P("snp", None, None),
        P("snp", None, None),
        P("snp", None, None),
        P(None, None, "snp"),
    )
    out_specs = (P(None, "snp"), P(None, "ppl"))
    return jax.shard_map(
        functools.partial(shards, people), mesh=mesh, in_specs=in_specs, out_specs=out_specs, check_vma=False
    )
```

```python
import functools

import jax
import jax.numpy as jnp
from jax import lax
from jax.experimental import pallas as pl
from jax.experimental.pallas import tpu as pltpu
from jax.sharding import PartitionSpec as P

F32 = jnp.float32
BF16 = jnp.bfloat16
MESH = pl.DeviceIdType.MESH
HIGHEST = lax.Precision.HIGHEST
FACTORS = (0.0, 0.3, 0.6, 1.0)
TRAITS, ROWS, SNPS, BLOCK, NB = 64, 3840, 1024, 128, 8
TILES = 32
FAR_FIRST = (6, 2, 5, 7, 4, 1, 3)
PAIRS = (
    [(p, q) for q in range(1, 4) for p in range(q)],
    [(p, q) for q in range(5, 8) for p in range(4, q)],
    [(p, q) for q in range(4, 8) for p in range(4)],
)


def ds(start, size):
    return pl.ds(pl.multiple_of(start, size), size)


def dot(a, b):
    return jnp.dot(a, b, preferred_element_type=F32)


def dot_nt(a, b, precision=None):
    return lax.dot_general(a, b, (((1,), (1,)), ((), ())), precision=precision, preferred_element_type=F32)


def dot_tn(a, b):
    return lax.dot_general(a, b, (((0,), (0,)), ((), ())), preferred_element_type=F32)


def split(x):
    high = x.astype(BF16)
    return high, (x - high.astype(F32)).astype(BF16)


def stacked(x):
    return jnp.concatenate(split(x), axis=0)


def dot3(a, b_high, b_low):
    n = a.shape[0]
    high, low = split(a)
    both = dot(jnp.concatenate([high, low], axis=0), b_high)
    return both[:n] + both[n:] + dot(high, b_low)


def kernel(
    people,
    x_hbm, r_hbm, e_hbm, a_ref, ld_hbm, inv_hbm, fac_hbm, n_hbm,
    e_out, r_out,
    xv, rv, ev, ldv, invv, facv, nv,
    rl, acc, rxs0, rxs1, rxs2, rxr0, rxr1, rxr2, rxl,
    gram_a, gram_b, gram_c, gr_a, gr_b, gr_c, gy_c, gs_c, ms_a, ms_b, ms_c, mr_a, mr_b, mr_c, gch, gcl, mh, ml, wh, wl, jit, lin,
    mine, everyone, chl, d, cr, yr, zr, rn,
    send_sem, recv_sem, local_sem,
):
    me = lax.axis_index("ppl")
    snp = lax.axis_index("snp")
    yh, xx = me // 4, lax.rem(me, 4)
    yl, zz, cc = snp // 16, lax.rem(snp // 2, 8), lax.rem(snp, 2)

    def on_ppl(j):
        return {"ppl": lax.rem(yh + j // 4, 2) * 4 + lax.rem(xx + j % 4, 4), "snp": snp}

    def on_z(j):
        return {"ppl": me, "snp": yl * 16 + lax.rem(zz + j, 8) * 2 + cc}

    on_y = {"ppl": me, "snp": (1 - yl) * 16 + zz * 2 + cc}
    on_core = {"ppl": me, "snp": yl * 16 + zz * 2 + 1 - cc}

    sends = []
    count = [0]

    def slots(n):
        first = count[0]
        count[0] += n
        return first

    def copy(src, dst, slot, device):
        return pltpu.make_async_remote_copy(
            src_ref=src, dst_ref=dst, send_sem=send_sem.at[slot], recv_sem=recv_sem.at[slot],
            device_id=device, device_id_type=MESH,
        )

    def start(src, dst, slot, device):
        c = copy(src, dst, slot, device)
        c.start()
        sends.append(c)
        return c

    def ppl_scatter(src_of, dst):
        base = slots(7)
        return [start(src_of(on_ppl(j)["ppl"]), dst.at[j - 1], base + j - 1, on_ppl(j)) for j in FAR_FIRST]

    def ppl_gather(src, dst):
        base = slots(7)
        return [start(src, dst, base + j - 1, on_ppl(j)) for j in FAR_FIRST]

    def arrived(copies):
        for c in copies:
            c.wait_recv()

    def load(i, src, dst):
        c = pltpu.make_async_copy(src, dst, local_sem.at[i])
        c.start()
        return c

    load_r = load(0, r_hbm, rv.at[:, 0:ROWS])
    load_x = []
    for g in range(4):
        top = min(1024 * g + 1024, ROWS)
        part = pl.ds(1024 * g, top - 1024 * g)
        load_x.append(load(1 + g, x_hbm.at[part, :], xv.at[part, :]))
    load_small = [
        load(5, inv_hbm, invv), load(6, fac_hbm, facv), load(7, n_hbm.at[:, ds(8 * me, 8), :], nv),
        load(8, ld_hbm, ldv), load(9, e_hbm, ev),
    ]
    xv[ROWS:4096, :] = jnp.zeros((4096 - ROWS, SNPS), BF16)
    rv[:, ROWS:4096] = jnp.zeros((TRAITS, 4096 - ROWS), F32)

    barrier = pltpu.get_barrier_semaphore()
    partners = [on_ppl(j) for j in range(1, 8)] + [on_z(j) for j in range(1, 8)] + [on_y, on_core]
    for device in partners:
        pl.semaphore_signal(barrier, 1, device_id=device, device_id_type=MESH)

    load_r.wait()
    squares = jnp.zeros((TRAITS, BLOCK), F32)
    for g in range(4):
        x = rv[:, 1024 * g:1024 * g + 1024]
        rl[g] = stacked(x)
        for i in range(8):
            t = x[:, i * 128:i * 128 + 128]
            squares = squares + t * t
    for g in range(4):
        load_x[g].wait()
        v = dot(rl[g], xv[1024 * g:1024 * g + 1024, :])
        if g == 0:
            acc[...] = v
        else:
            acc[...] += v
    rxs0[:, 0:512] = acc[0:64, 0:512] + acc[64:128, 0:512]
    rxs0[:, 512:640] = squares
    rxl[...] = acc[0:64, 512:1024] + acc[64:128, 512:1024]

    def gram(buf, pairs, first, last):
        for q in range(first, last):
            rows = [p for p, other in pairs if other == q]
            if q % 2 == 0 and rows and (rows[0], q + 1) in pairs:
                continue
            wide = 2 if q % 2 == 1 and (rows[0], q - 1) in pairs else 1
            left = q + 1 - wide
            v = dot_tn(xv[0:ROWS, rows[0] * 128:rows[-1] * 128 + 128], xv[0:ROWS, left * 128:q * 128 + 128])
            for w in range(wide):
                for p in rows:
                    if (p, left + w) in pairs:
                        buf[pairs.index((p, left + w))] = v[(p - rows[0]) * 128:(p - rows[0]) * 128 + 128, w * 128:w * 128 + 128]

    gram(gram_a, PAIRS[0], 1, 4)
    pl.semaphore_wait(barrier, len(partners))
    rs0 = ppl_scatter(lambda to: rxs0.at[ds(8 * to, 8), :], rxr0)
    rs_a = ppl_scatter(lambda to: gram_a.at[:, ds(16 * to, 16), :], gr_a)

    for c in load_small:
        c.wait()
    shrink = jnp.zeros((NB, BLOCK), F32)
    for component, factor in enumerate(FACTORS):
        shrink = shrink + jnp.where(a_ref[...] == component, F32(factor), F32(0.0))
    mine_rows = ds(8 * me, 8)
    e_mine = ev[mine_rows, :]
    for q in range(NB):
        col = slice(q * 128, q * 128 + 128)
        scale = shrink[q:q + 1, :]
        w_high, w_low = split(invv[q] * scale)
        wh[q] = w_high
        wl[q] = w_low
        noise = jnp.concatenate([nv[0, :, col], nv[1, :, col]], axis=0)
        jit[:, col] = dot_nt(noise, facv[q], HIGHEST) * scale

    def linear(beta):
        for q in range(NB):
            col = slice(q * 128, q * 128 + 128)
            lin[:, col] = jnp.dot(beta[:, col], ldv[q], precision=HIGHEST, preferred_element_type=F32)

    linear(e_mine)

    gram(gram_b, PAIRS[1], 5, 8)
    cross = dot_tn(xv[0:ROWS, 0:512], xv[0:ROWS, 512:1024])
    for i, (p, q) in enumerate(PAIRS[2]):
        gram_c[i] = cross[p * 128:p * 128 + 128, (q - 4) * 128:(q - 4) * 128 + 128]
    high, low = split(cross)
    gch[...] = high
    gcl[...] = low

    def received(rxs, rxr, copies):
        arrived(copies)
        total = rxs[mine_rows, :]
        for j in range(7):
            total = total + rxr[j]
        return total

    def spread_of(sums):
        return jnp.sqrt(jnp.sum(sums, axis=1, keepdims=True) / people)

    def base_of(total, first, spread, sweep):
        out = []
        for i in range(total.shape[1] // 128):
            q = first + i
            col = slice(q * 128, q * 128 + 128)
            rhs = total[:, i * 128:i * 128 + 128] + lin[:, col]
            out.append(dot3(rhs, wh[q], wl[q]) + spread * jit[8 * sweep:8 * sweep + 8, col])
        return out

    def coupling(gram_ref, gr, copies, pairs, ms, mr):
        arrived(copies)
        rows = ds(16 * me, 16)
        total = gram_ref[:, rows, :]
        for j in range(7):
            total = total + gr[j]
        for q in sorted({q for _, q in pairs}):
            at = [i for i, (_, other) in enumerate(pairs) if other == q]
            v = dot3(total[at[0]:at[-1] + 1].reshape(len(at) * 16, 128), wh[q], wl[q]).reshape(len(at), 16, 128)
            ms[at[0]:at[-1] + 1] = v
            mr[at[0]:at[-1] + 1, rows, :] = v
        return ppl_gather(ms, mr.at[:, rows, :])

    def unpack(copies, pairs, mr):
        arrived(copies)
        for i, (p, q) in enumerate(pairs):
            m_high, m_low = split(mr[i])
            mh[p, :, q * 128:q * 128 + 128] = m_high
            ml[p, :, q * 128:q * 128 + 128] = m_low

    def chain(base, first, last, before, sweep):
        base = dict(zip(range(first, last), base))
        gathers = []
        for q in range(first, last):
            col = slice(q * 128, q * 128 + 128)
            new = base[q]
            mine[sweep, :, col] = new
            if q + 1 < last:
                high, low = split(new - before[:, col])
                both = dot(jnp.concatenate([high, low], axis=0), mh[q, :, (q + 1) * 128:last * 128])
                change = both[:8] + both[8:] + dot(high, ml[q, :, (q + 1) * 128:last * 128])
                for later in range(q + 1, last):
                    at = (later - q - 1) * 128
                    base[later] = base[later] - change[:, at:at + 128]
            if q % 4 == 3:
                span = pl.ds((q - 3) * 128, 512)
                everyone[sweep, mine_rows, span] = mine[sweep, :, span]
                gathers.append(ppl_gather(mine.at[sweep, :, span], everyone.at[sweep, mine_rows, span]))
        return gathers

    def changes(gather, sweep, half):
        arrived(gather)
        col = slice(half * 512, half * 512 + 512)
        before = ev[:, col] if sweep == 0 else everyone[0, :, col]
        both = stacked(everyone[sweep, :, col] - before)
        chl[sweep, half] = both
        return both

    def half_delta(sweep):
        @pl.loop(0, 4)
        def _(g):
            v = dot_nt(chl[sweep, 0], xv[ds(g * 1024, 1024), 0:512])
            for i in range(8):
                col = slice(i * 128, i * 128 + 128)
                d[sweep, g * 8 + i] = v[0:64, col] + v[64:128, col]

    def reduce_residual(sweep, own_residual, *between):
        far_first, near_first = (4, 3, 5, 2, 6, 1, 7, 0), (1, 7, 2, 6, 3, 5, 4)
        theirs = (1 - cc) * 16
        own = cc * 16
        far = own + 8 * (1 - yl)
        near = own + 8 * yl
        core_slot, y_slot, z_slot = slots(9), slots(8), slots(7)

        def finish(first):
            v = dot_nt(chl[sweep, 1], xv[ds(first * 128, 1024), 512:1024])
            for i in range(8):
                col = slice(i * 128, i * 128 + 128)
                d[sweep, first + i] += v[0:64, col] + v[64:128, col]

        finish(theirs + 8 * (1 - yl))
        core, to_y, to_z = {}, {}, {}
        for k in far_first:
            z = lax.rem(zz + k, 8)
            core[k] = start(d.at[sweep, theirs + 8 * (1 - yl) + z], cr.at[sweep, 0, k], core_slot + k, on_core)
        finish(far)
        for k in far_first:
            z = lax.rem(zz + k, 8)
            core[k].wait_recv()
            d[sweep, far + z] += cr[sweep, 0, k]
            to_y[k] = start(d.at[sweep, far + z], yr.at[sweep, k], y_slot + k, on_y)
        finish(theirs + 8 * yl)
        second = start(d.at[sweep, ds(theirs + 8 * yl, 8)], cr.at[sweep, 1], core_slot + 8, on_core)
        finish(near)
        second.wait_recv()
        for i in range(8):
            d[sweep, near + i] += cr[sweep, 1, i]
        for k in far_first[:7]:
            to_y[k].wait_recv()
            z = lax.rem(zz + k, 8)
            d[sweep, near + z] += yr[sweep, k]
            to_z[k] = start(d.at[sweep, near + z], zr.at[sweep, k - 1], z_slot + k - 1, on_z(k))
        if between:
            between[0]()
        to_y[0].wait_recv()
        total = d[sweep, near + zz] + yr[sweep, 0]
        for k in far_first[:7]:
            to_z[k].wait_recv()
            total = total + zr[sweep, k - 1]
        rn[sweep, near + zz] = own_residual(near + zz) - total

        z_slot, y_slot, near_slot, far_slot = slots(7), slots(8), slots(8), slots(8)
        mine_at = rn.at[sweep, near + zz]
        from_z, from_y, from_core, last = {}, {}, {}, {}
        from_y[0] = start(mine_at, mine_at, y_slot, on_y)
        for k in (4, 1, 7, 2, 6, 3, 5):
            from_z[k] = start(mine_at, mine_at, z_slot + k - 1, on_z(k))
        from_core[0] = start(mine_at, mine_at, near_slot, on_core)
        if between:
            between[1]()
        for k in near_first:
            from_z[k].wait_recv()
            tile = rn.at[sweep, near + lax.rem(zz + 8 - k, 8)]
            from_y[k] = start(tile, tile, y_slot + k, on_y)
            from_core[k] = start(tile, tile, near_slot + k, on_core)
        yield near // 8
        for k in (0,) + near_first:
            from_y[k].wait_recv()
            tile = rn.at[sweep, far + lax.rem(zz + 8 - k, 8)]
            last[k] = start(tile, tile, far_slot + k, on_core)
        yield far // 8
        arrived(from_core.values())
        yield (theirs + 8 * yl) // 8
        arrived(last.values())
        yield (theirs + 8 * (1 - yl)) // 8

    total = received(rxs0, rxr0, rs0)
    spread = spread_of(total[:, 512:640])
    base = base_of(total[:, 0:512], 0, spread, 0)
    ag_a = coupling(gram_a, gr_a, rs_a, PAIRS[0], ms_a, mr_a)
    rs_b = ppl_scatter(lambda to: gram_b.at[:, ds(16 * to, 16), :], gr_b)
    unpack(ag_a, PAIRS[0], mr_a)
    gather, = chain(base, 0, 4, e_mine, 0)
    both = changes(gather, 0, 0)
    v = dot(both, gch[...])
    rxs1[...] = rxl[...] - (v[0:64] + v[64:128] + dot(both[0:64], gcl[...]))
    rs1 = ppl_scatter(lambda to: rxs1.at[ds(8 * to, 8), :], rxr1)
    ag_b = coupling(gram_b, gr_b, rs_b, PAIRS[1], ms_b, mr_b)
    half_delta(0)
    total = received(rxs1, rxr1, rs1)
    base = base_of(total, 4, spread, 0)
    unpack(ag_b, PAIRS[1], mr_b)
    gather, = chain(base, 4, 8, e_mine, 0)

    rows = ds(32 * xx, 32)
    pending = {}

    def on_x(j):
        return {"ppl": yh * 4 + lax.rem(xx + j, 4), "snp": snp}

    def cross_scatter():
        base = slots(3)
        pending["x"] = [
            start(gram_c.at[:, ds(32 * lax.rem(xx + j, 4), 32), :], gr_c.at[j - 1], base + j - 1, on_x(j)) for j in (2, 1, 3)
        ]

    def cross_sum():
        arrived(pending["x"])
        gs_c[...] = gram_c[:, rows, :] + gr_c[0] + gr_c[1] + gr_c[2]
        pending["y"] = [start(gs_c, gy_c, slots(1), on_ppl(4))]

    def cross_coupling():
        arrived(pending["y"])
        for q in range(4, 8):
            at = slice((q - 4) * 4, (q - 4) * 4 + 4)
            v = dot3((gs_c[at] + gy_c[at]).reshape(128, 128), wh[q], wl[q]).reshape(4, 32, 128)
            ms_c[at] = v
            mr_c[at, rows, :] = v
        base = slots(3)
        pending["m"] = [start(ms_c, mr_c.at[:, rows, :], base + j - 1, on_x(j)) for j in (2, 1, 3)]

    cross_scatter()
    changes(gather, 0, 1)
    squares = jnp.zeros((TRAITS, BLOCK), F32)
    for step, group in enumerate(reduce_residual(0, lambda tile: rv[:, ds(tile * 128, 128)], cross_sum, cross_coupling)):
        tiles = [rn[0, group * 8 + i] for i in range(8)]
        for t in tiles:
            squares = squares + t * t
        v = dot(stacked(jnp.concatenate(tiles, axis=1)), xv[ds(group * 1024, 1024), :])
        if step == 0:
            acc[...] = v
        else:
            acc[...] += v
    rxs2[:, 0:1024] = acc[0:64, :] + acc[64:128, :]
    rxs2[:, 1024:1152] = squares
    rs2 = ppl_scatter(lambda to: rxs2.at[ds(8 * to, 8), :], rxr2)
    linear(mine[0])

    total = received(rxs2, rxr2, rs2)
    base = base_of(total[:, 0:1024], 0, spread_of(total[:, 1024:1152]), 1)
    first_gather, = chain(base[0:4], 0, 4, mine[0], 1)
    unpack(pending["m"], PAIRS[2], mr_c)
    high, low = split(mine[1, :, 0:512] - mine[0, :, 0:512])
    both = dot(jnp.concatenate([high, low], axis=0), mh[0:4, :, 512:1024].reshape(512, 512))
    change = both[:8] + both[8:] + dot(high, ml[0:4, :, 512:1024].reshape(512, 512))
    later = [base[4 + i] - change[:, i * 128:i * 128 + 128] for i in range(4)]
    second_gather, = chain(later, 4, 8, mine[0], 1)
    changes(first_gather, 1, 0)
    half_delta(1)
    changes(second_gather, 1, 1)
    e_out[...] = everyone[1]
    copies = []
    for group in reduce_residual(1, lambda tile: rn[0, tile]):
        for i in range(8):
            tile = group * 8 + i
            copies.append(pltpu.make_async_copy(rn.at[1, tile], r_out.at[:, ds(tile * 128, 128)], local_sem.at[len(copies)]))
            copies[-1].start()
    for c in copies:
        c.wait()
    for c in sends:
        c.wait_send()


def deliver(e_ref, r_ref, e_out, r_out):
    e_out[...] = e_ref[...]
    r_out[...] = r_ref[:, 0:ROWS]


def shards(people, genotypes, residual, effects, assignments, ld_blocks, ld_inverses, ld_factors, normals):
    hbm = pl.BlockSpec(memory_space=pl.ANY)
    vmem = pl.BlockSpec(memory_space=pltpu.VMEM)
    wide = (NB, BLOCK, BLOCK)
    scratch = [
        ((4096, SNPS), BF16), ((TRAITS, 4096), F32), ((TRAITS, SNPS), F32), (wide, F32), (wide, F32), (wide, F32),
        ((2, 8, SNPS), F32),
        ((4, 128, 1024), BF16), ((128, 1024), F32),
        ((TRAITS, 640), F32), ((TRAITS, 512), F32), ((TRAITS, 1152), F32),
        ((7, 8, 640), F32), ((7, 8, 512), F32), ((7, 8, 1152), F32), ((TRAITS, 512), F32),
    ]
    scratch += [((len(p), BLOCK, BLOCK), F32) for p in PAIRS]
    cross = (len(PAIRS[2]), 32, BLOCK)
    scratch += [((7, len(p), 16, BLOCK), F32) for p in PAIRS[:2]] + [((3, *cross), F32), (cross, F32), (cross, F32)]
    scratch += [((len(p), 16, BLOCK), F32) for p in PAIRS[:2]] + [(cross, F32)]
    scratch += [((len(p), BLOCK, BLOCK), F32) for p in PAIRS]
    scratch += [
        ((512, 512), BF16), ((512, 512), BF16), ((NB, BLOCK, SNPS), BF16), ((NB, BLOCK, SNPS), BF16),
        (wide, BF16), (wide, BF16), ((16, SNPS), F32), ((8, SNPS), F32),
        ((2, 8, SNPS), F32), ((2, TRAITS, SNPS), F32), ((2, 2, 128, 512), BF16),
        ((2, TILES, TRAITS, 128), F32), ((2, 2, 8, TRAITS, 128), F32), ((2, 8, TRAITS, 128), F32),
        ((2, 7, TRAITS, 128), F32), ((2, TILES, TRAITS, 128), F32),
    ]
    slots = 3 * 7 + 2 * 7 + 2 * 7 + 7 + 4 * 7 + 2 * (9 + 8 + 7 + 7 + 8 + 8 + 8)
    e_new, r_new = pl.pallas_call(
        functools.partial(kernel, people),
        out_shape=(
            jax.ShapeDtypeStruct(effects.shape, F32),
            jax.ShapeDtypeStruct((TRAITS, TILES * 128), F32),
        ),
        in_specs=[hbm, hbm, hbm, vmem, hbm, hbm, hbm, hbm],
        out_specs=(vmem, hbm),
        scratch_shapes=[pltpu.VMEM(shape, dtype) for shape, dtype in scratch]
        + [pltpu.SemaphoreType.DMA((slots,)), pltpu.SemaphoreType.DMA((slots,)), pltpu.SemaphoreType.DMA((33,))],
        compiler_params=pltpu.CompilerParams(collective_id=0, has_side_effects=True, vmem_limit_bytes=58 << 20),
        cost_estimate=pl.CostEstimate(flops=20_000_000_000, bytes_accessed=16_000_000, transcendentals=0),
        name="gibbs_sweeps",
    )(genotypes, residual, effects, assignments.reshape(NB, BLOCK), ld_blocks, ld_inverses, ld_factors, normals)
    return pl.pallas_call(
        deliver,
        out_shape=(jax.ShapeDtypeStruct(effects.shape, F32), jax.ShapeDtypeStruct(residual.shape, F32)),
        in_specs=[vmem, vmem],
        out_specs=(vmem, vmem),
        name="deliver",
    )(e_new, r_new)


def solution(mesh):
    people = ROWS * mesh.shape["ppl"]
    in_specs = (
        P("ppl", "snp"),
        P(None, "ppl"),
        P(None, "snp"),
        P("snp"),
        P("snp", None, None),
        P("snp", None, None),
        P("snp", None, None),
        P(None, None, "snp"),
    )
    out_specs = (P(None, "snp"), P(None, "ppl"))
    return jax.shard_map(
        functools.partial(shards, people), mesh=mesh, in_specs=in_specs, out_specs=out_specs, check_vma=False
    )
```
